32 devices in a mesh: grp: 8 (over y, x, core), frq: 4 (over z).
Axes of the slice: x: 2, y: 2, z: 4, core: 2. Of those that a mesh axis runs over, the one named last changes fastest.
Arguments:
- spectra: bfloat16 [8, 512, 240, 128], P('grp', 'frq'), may hold values from -6 to 6
- band_weight: float32 [512], replicated, may hold values from 0.25 to 4
Outputs:
- correlations: bfloat16 [2, 8, 4096, 1024], P(None, 'grp', 'frq')
The draws below stay inside these ranges and needn't reach their ends.
All inputs are finite; a program needn't handle non-finite values.
Results may differ from the reference program's by a relative error of at most 0.0058.
Values may be sent and summed in bfloat16 or wider, within the bound.
No kernel may reach another device: no remote copies, remote signals or barrier semaphores. Data moves between devices by JAX's collectives and lax.ppermute only.
A program may use at most 64 MiB of HBM per device.

```python
import math
import jax
import jax.numpy as jnp
from jax import lax

STA = 64
FREQS = 512
WIN = 240
ROUNDS = 2
GROUPS = 8


def steps_of(own_key, dims, pieces, least, high):
    factor_of = 1.0
    for axis_at, shards_of in pieces:
        heights = jax.random.uniform(jax.random.fold_in(jax.random.fold_in(own_key, 6), axis_at), (shards_of,), jnp.float32, least / len(pieces), high / len(pieces))
        factor_of = factor_of * jnp.repeat(jnp.exp(heights), dims[axis_at] // shards_of).reshape((-1,) + (1,) * (len(dims) - 1 - axis_at))
    return factor_of


def bell_draw(key, extent, width, reach, cuts=(), kind=jnp.bfloat16):
    level = steps_of(key, extent, cuts, -0.22, 0.18) if cuts else 1.0
    array = jax.random.normal(key, extent, jnp.float32) * width * level
    return jnp.minimum(jnp.maximum(array, -reach), reach).astype(kind)


def setup_inputs(seed: int = 0) -> dict:
    arg_keys = jax.random.split(jax.random.key(seed), 3)
    spectra = bell_draw(arg_keys[0], (GROUPS, FREQS, WIN, 2 * STA), 1.0, 6.0, ((0, 8), (1, 4)))
    band_weight = jnp.clip(jnp.exp(jax.random.uniform(arg_keys[1], (FREQS,), jnp.float32, math.log(0.25), math.log(4.0))), 0.25, 4.0)
    return {"spectra": spectra, "band_weight": band_weight}


def inverse_table(band_weight):
    bin_count = band_weight.shape[0]
    lag_count = 2 * bin_count
    phase_index = jnp.arange(bin_count, dtype=jnp.int32)[:, None] * jnp.arange(lag_count, dtype=jnp.int32)[None, :] % lag_count
    phase_angle = phase_index.astype(jnp.float32) * (2.0 * math.pi / lag_count)
    weighting = band_weight[:, None] * (1.0 / math.sqrt(bin_count))
    return jnp.stack([weighting * jnp.cos(phase_angle), -weighting * jnp.sin(phase_angle)], 1).astype(jnp.bfloat16)

def cross_stack(local_block, partner_block):
    windows = local_block.shape[1]
    half_width = local_block.shape[2] // 2
    product = jnp.einsum('fwa,fwb->fab', local_block.astype(jnp.float32), partner_block.astype(jnp.float32))
    real_part = product[:, :half_width, :half_width] + product[:, half_width:, half_width:]
    imag_part = product[:, half_width:, :half_width] - product[:, :half_width, half_width:]
    scaled = jnp.stack([real_part, imag_part], 1) * (1.0 / math.sqrt(windows))
    return scaled.reshape(scaled.shape[0], 2, half_width * half_width).astype(jnp.bfloat16)

def reference(spectra, band_weight):
    lag_table = inverse_table(band_weight).astype(jnp.float32)
    group_count = spectra.shape[0]
    outputs = []
    for turn_index in range(ROUNDS):
        offset = turn_index + 1

        def one_group(group_id):
            local_block = lax.dynamic_index_in_dim(spectra, group_id, 0, keepdims=False)
            partner_id = ((group_id - offset) % group_count).astype(jnp.int32)
            partner_block = lax.dynamic_index_in_dim(spectra, partner_id, 0, keepdims=False)
            stacked = cross_stack(local_block, partner_block)
            lagged = jnp.einsum('fcp,fcl->pl', stacked.astype(jnp.float32), lag_table)
            return lagged.astype(jnp.bfloat16)
        outputs.append(lax.map(one_group, jnp.arange(group_count, dtype=jnp.int32)))
    return jnp.stack(outputs)
```

```python
import functools
import math

import jax
import jax.numpy as jnp
from jax import lax
from jax.experimental import pallas as pl
from jax.experimental.pallas import tpu as pltpu
from jax.sharding import PartitionSpec as P

ROUNDS = 2
CHUNK = 16


def permuted(value, target):
    count = lax.axis_size("grp")
    return lax.ppermute(value, "grp", [(source, target(source) % count) for source in range(count)])


def is_odd(group):
    return (group // 2) % 2


def to_x(group):
    return group ^ 2


def to_y(group):
    return group + 4 if is_odd(group) else group - 4


def to_b(group):
    return group if is_odd(group) else group + 4


def to_other_core(group):
    return group ^ 1


def cross_body(shards, step_freqs, scalars, own, x_mine, y_mine, x_other, last_other, out, stage):
    windows, width = own.shape[1:]
    half = width // 2
    freqs = out.shape[4]
    per_shard = half // shards
    step = pl.program_id(0)
    first_core = scalars[0] == 0
    odd = scalars[1] == 1
    scale = 1.0 / math.sqrt(windows)
    lanes = lax.broadcasted_iota(jnp.int32, (half, width), 1)
    sign = jnp.where(lanes < half, 1.0, -1.0).astype(jnp.float32)

    def products(left, rights):
        return lax.dot_general(
            left,
            jnp.concatenate(rights, 1),
            (((0,), (0,)), ((), ())),
            preferred_element_type=jnp.float32,
        )

    for at in range(step_freqs):
        center, center_other, other = x_mine[at], x_other[at], last_other[at]
        before = jnp.where(odd, y_mine[at], own[at])
        after = jnp.where(odd, own[at], y_mine[at])
        pair = [
            products(center, [jnp.where(first_core, other, center_other), before]),
            products(after, [jnp.where(first_core, center_other, other), center]),
        ]
        for bundle, product in enumerate(pair):
            for turn in range(ROUNDS):
                part = product[:, turn * width : (turn + 1) * width]
                top, bottom = part[:half], part[half:]
                value = (top * sign + pltpu.roll(bottom, half, 1)) * scale
                base = (bundle * ROUNDS + turn) * half * freqs
                stage[pl.ds(base + step * step_freqs + at, half, stride=freqs), :] = value

    @pl.when(step == pl.num_programs(0) - 1)
    def _():
        for bundle in range(2):
            for turn in range(ROUNDS):
                for shard in range(shards):
                    base = ((bundle * ROUNDS + turn) * half + shard * per_shard) * freqs
                    rows = stage[pl.ds(base, per_shard * freqs), :]
                    out[shard, bundle, turn] = rows.reshape(per_shard, freqs, width).astype(out.dtype)


def cross_spectra(scalars, spectra, x_mine, y_mine, x_other, last_other, shards):
    freqs, windows, width = x_mine.shape
    step_freqs = math.gcd(freqs, 4)
    half = width // 2
    block = (step_freqs, windows, width)
    plain = pl.BlockSpec(block, lambda step, scalars: (step, 0, 0))
    out_shape = (shards, 2, ROUNDS, half // shards, freqs, width)
    return pl.pallas_call(
        functools.partial(cross_body, shards, step_freqs),
        out_shape=jax.ShapeDtypeStruct(out_shape, jnp.bfloat16),
        grid_spec=pltpu.PrefetchScalarGridSpec(
            num_scalar_prefetch=1,
            grid=(freqs // step_freqs,),
            in_specs=[
                pl.BlockSpec(block, lambda step, scalars: (scalars[2] * (freqs // step_freqs) + step, 0, 0))
            ]
            + [plain] * 4,
            out_specs=pl.BlockSpec(out_shape, lambda step, scalars: (0,) * 6),
            scratch_shapes=[pltpu.VMEM((2 * ROUNDS * half * freqs, width), jnp.float32)],
        ),
        compiler_params=pltpu.CompilerParams(vmem_limit_bytes=48 * 1024 * 1024),
        cost_estimate=pl.CostEstimate(
            flops=2 * freqs * 2 * windows * width * 2 * width,
            bytes_accessed=5 * freqs * windows * width * 2 + 4 * freqs * half * width * 2,
            transcendentals=0,
        ),
    )(scalars, spectra, x_mine, y_mine, x_other, last_other)


def lag_body(count, *refs):
    blocks, table, out = refs[:count], refs[count], refs[count + 1]
    shards, _, stations, _, width = blocks[0].shape
    half = width // 2
    rows = []
    for station in range(stations):
        spectrum = jnp.concatenate(
            [block[shard, 0, station] for block in blocks for shard in range(shards)], 0
        )
        turned = spectrum.T
        rows.append(jnp.concatenate([turned[:half], turned[half:]], 1))
    left = jnp.concatenate(rows, 0)
    out[0, 0] = jnp.dot(left, table[...], preferred_element_type=jnp.float32).astype(out.dtype)


def to_lags(blocks, table):
    shards, rounds, stations, freqs, width = blocks[0].shape
    half = width // 2
    depth, lags = table.shape
    step = math.gcd(stations, 4)
    block = pl.BlockSpec((shards, 1, step, freqs, width), lambda turn, at: (0, turn, at, 0, 0))
    return pl.pallas_call(
        functools.partial(lag_body, len(blocks)),
        out_shape=jax.ShapeDtypeStruct((rounds, 1, stations * half, lags), jnp.bfloat16),
        grid=(rounds, stations // step),
        in_specs=[block] * len(blocks) + [pl.BlockSpec((depth, lags), lambda turn, at: (0, 0))],
        out_specs=pl.BlockSpec((1, 1, step * half, lags), lambda turn, at: (turn, 0, at, 0)),
        compiler_params=pltpu.CompilerParams(vmem_limit_bytes=48 * 1024 * 1024),
        cost_estimate=pl.CostEstimate(
            flops=2 * rounds * stations * half * depth * lags,
            bytes_accessed=2 * (rounds * stations * half * (depth + lags) + depth * lags),
            transcendentals=0,
        ),
    )(*blocks, table)


def inverse_table(band_weight, halves, chunks):
    bins = band_weight.shape[0]
    shards = lax.axis_size("frq")
    lags = 2 * bins
    size = bins // (shards * 2 * chunks)
    dims = (chunks, 2, shards, size)
    weights = band_weight.reshape(shards, 2, chunks, size)
    weights = jnp.where(halves[0] == 0, weights, weights[:, ::-1]).transpose(2, 1, 0, 3).reshape(bins)
    indices = lax.broadcasted_iota(jnp.int32, dims, 2) * (2 * chunks * size)
    indices += (lax.broadcasted_iota(jnp.int32, dims, 1) ^ halves[0]) * (chunks * size)
    indices += lax.broadcasted_iota(jnp.int32, dims, 0) * size
    indices += lax.broadcasted_iota(jnp.int32, dims, 3)
    indices = indices.reshape(bins)
    phase_index = indices[:, None] * jnp.arange(lags, dtype=jnp.int32)[None, :] % lags
    phase_angle = phase_index.astype(jnp.float32) * (2.0 * math.pi / lags)
    weighting = weights[:, None] * (1.0 / math.sqrt(bins))
    table = jnp.stack(
        [weighting * jnp.cos(phase_angle), -weighting * jnp.sin(phase_angle)], 0
    ).astype(jnp.bfloat16)
    return table.reshape(2 * bins, lags)


def local(spectra, band_weight):
    shards = lax.axis_size("frq")
    group = lax.axis_index("grp").astype(jnp.int32)
    core, odd = group & 1, (group >> 1) & 1
    block = spectra[0]
    half_size = block.shape[0] // 2
    chunks = max(1, half_size // CHUNK)
    size = half_size // chunks

    def piece(source, half, chunk):
        return lax.dynamic_slice_in_dim(source, (half * chunks + chunk) * size, size, 0)

    source = block
    sent = []
    for chunk in range(chunks):
        x_piece, y_piece = piece(source, 1 - odd, chunk), piece(source, odd, chunk)
        if chunk == 0:
            x_piece, y_piece, source = lax.optimization_barrier((x_piece, y_piece, source))
        sent.append((x_piece, y_piece, permuted(x_piece, to_x), permuted(y_piece, to_y)))

    blocks = []
    for chunk, (_, own, x_mine, y_mine) in enumerate(sent):
        x_other = permuted(x_mine, to_other_core)
        last_other = permuted(jnp.where(odd == core, y_mine, own), to_other_core)
        scalars = jnp.stack([core, odd, odd * chunks + chunk])
        result = cross_spectra(scalars, source, x_mine, y_mine, x_other, last_other, shards)
        spread = lax.all_to_all(result, "frq", split_axis=0, concat_axis=0, tiled=True)
        blocks += [permuted(spread[:, 0], to_x), permuted(spread[:, 1], to_b)]

    table = inverse_table(band_weight, [1 - odd, odd], chunks)
    return to_lags(blocks, table)


def solution(mesh):
    return jax.shard_map(
        local,
        mesh=mesh,
        in_specs=(P("grp", "frq", None, None), P()),
        out_specs=P(None, "grp", "frq", None),
        check_vma=False,
    )
```

```python
import functools
import math

import jax
import jax.numpy as jnp
from jax import lax
from jax.experimental import pallas as pl
from jax.experimental.pallas import tpu as pltpu
from jax.sharding import PartitionSpec as P

ROUNDS = 2
CHUNK = 16
STRAIGHT = 1
VMEM = 48 * 1024 * 1024
LITTLE = 8 * 1024 * 1024


def permuted(value, target):
    count = lax.axis_size("grp")
    return lax.ppermute(value, "grp", [(source, target(source) % count) for source in range(count)])


def permuted_far(value, target, distance):
    groups, shards = lax.axis_size("grp"), lax.axis_size("frq")
    return lax.ppermute(
        value,
        ("grp", "frq"),
        [
            (group * shards + shard, (target(group) % groups) * shards + (shard + distance) % shards)
            for group in range(groups)
            for shard in range(shards)
        ],
    )


def is_odd(group):
    return (group // 2) % 2


def to_x(group):
    return group ^ 2


def to_y(group):
    return group + 4 if is_odd(group) else group - 4


def to_b(group):
    return group if is_odd(group) else group + 4


def to_other_core(group):
    return group ^ 1


def cross_body(shards, step_freqs, early, straight, scalars, own, x_mine, y_mine, x_other, last_other, *refs):
    outs, stage = refs[early:-1], refs[-1]
    windows, width = own.shape[1:]
    half = width // 2
    per_shard, freqs = outs[0].shape[-3:-1]
    step = pl.program_id(0)
    first_core = scalars[0] == 0
    odd = scalars[1] == 1
    scale = 1.0 / math.sqrt(windows)
    lanes = lax.broadcasted_iota(jnp.int32, (half, width), 1)
    sign = jnp.where(lanes < half, 1.0, -1.0).astype(jnp.float32)

    def products(left, rights):
        return lax.dot_general(
            left,
            jnp.concatenate(rights, 1),
            (((0,), (0,)), ((), ())),
            preferred_element_type=jnp.float32,
        )

    for at in range(step_freqs):
        center, center_other, other = x_mine[at], x_other[at], last_other[at]
        before = jnp.where(odd, y_mine[at], own[at])
        after = jnp.where(odd, own[at], y_mine[at])
        pair = [
            products(center, [jnp.where(first_core, other, center_other), before]),
            products(after, [jnp.where(first_core, center_other, other), center]),
        ]
        for bundle, product in enumerate(pair):
            for turn in range(ROUNDS):
                part = product[:, turn * width : (turn + 1) * width]
                top, bottom = part[:half], part[half:]
                value = (top * sign + pltpu.roll(bottom, half, 1)) * scale
                base = (bundle * ROUNDS + turn) * half * freqs
                stage[pl.ds(base + step * step_freqs + at, half, stride=freqs), :] = value

    @pl.when(step == pl.num_programs(0) - 1)
    def _():
        for index in range(shards):
            shard = lax.rem(scalars[3] + index, shards) if straight else index
            for bundle in range(2):
                for turn in range(ROUNDS):
                    base = ((bundle * ROUNDS + turn) * half + shard * per_shard) * freqs
                    if straight:
                        base = pl.multiple_of(base, 8)
                    rows = stage[pl.ds(base, per_shard * freqs), :]
                    rows = rows.reshape(per_shard, freqs, width).astype(jnp.bfloat16)
                    if straight:
                        outs[bundle * shards + index][turn] = rows
                    else:
                        outs[0][index, bundle, turn] = rows


def cross_spectra(scalars, spectra, x_mine, y_mine, x_other, last_other, earlier, shards, straight):
    freqs, windows, width = x_mine.shape
    step_freqs = math.gcd(freqs, 4)
    half = width // 2
    block = (step_freqs, windows, width)
    plain = pl.BlockSpec(block, lambda step, scalars: (step, 0, 0))
    out_shape = (ROUNDS, half // shards, freqs, width)
    if not straight:
        out_shape = (shards, 2) + out_shape
    count = 2 * shards if straight else 1
    return pl.pallas_call(
        functools.partial(cross_body, shards, step_freqs, len(earlier), straight),
        out_shape=[jax.ShapeDtypeStruct(out_shape, jnp.bfloat16)] * count,
        grid_spec=pltpu.PrefetchScalarGridSpec(
            num_scalar_prefetch=1,
            grid=(freqs // step_freqs,),
            in_specs=[
                pl.BlockSpec(block, lambda step, scalars: (scalars[2] * (freqs // step_freqs) + step, 0, 0))
            ]
            + [plain] * 4
            + in_hbm(len(earlier)),
            out_specs=[pl.BlockSpec(out_shape, lambda step, scalars: (0,) * len(out_shape))] * count,
            scratch_shapes=[pltpu.VMEM((2 * ROUNDS * half * freqs, width), jnp.float32)],
        ),
        compiler_params=pltpu.CompilerParams(vmem_limit_bytes=VMEM),
        cost_estimate=pl.CostEstimate(
            flops=2 * freqs * 2 * windows * width * 2 * width,
            bytes_accessed=5 * freqs * windows * width * 2 + 4 * freqs * half * width * 2,
            transcendentals=0,
        ),
    )(scalars, spectra, x_mine, y_mine, x_other, last_other, *earlier)


def in_hbm(count):
    return [pl.BlockSpec(memory_space=pltpu.HBM)] * count


def last_body(scalars, own, y_mine, *refs):
    refs[-1][...] = jnp.where(scalars[0] == scalars[1], y_mine[...], own[...])


def last_after(scalars, own, y_mine, waits):
    return pl.pallas_call(
        last_body,
        out_shape=jax.ShapeDtypeStruct(y_mine.shape, jnp.bfloat16),
        in_specs=[pl.BlockSpec(memory_space=pltpu.SMEM)]
        + [pl.BlockSpec(memory_space=pltpu.VMEM)] * 2
        + in_hbm(len(waits)),
        out_specs=pl.BlockSpec(memory_space=pltpu.VMEM),
        compiler_params=pltpu.CompilerParams(vmem_limit_bytes=LITTLE),
        cost_estimate=pl.CostEstimate(flops=0, bytes_accessed=6 * y_mine.size, transcendentals=0),
    )(scalars, own, y_mine, *waits)


def bundles_body(spread, *refs):
    for bundle in range(2):
        refs[-2 + bundle][...] = spread[:, bundle]


def bundles_after(spread, waits):
    shape = jax.ShapeDtypeStruct(spread.shape[:1] + spread.shape[2:], spread.dtype)
    return pl.pallas_call(
        bundles_body,
        out_shape=[shape] * 2,
        in_specs=[pl.BlockSpec(memory_space=pltpu.VMEM)] + in_hbm(len(waits)),
        out_specs=[pl.BlockSpec(memory_space=pltpu.VMEM)] * 2,
        compiler_params=pltpu.CompilerParams(vmem_limit_bytes=LITTLE),
        cost_estimate=pl.CostEstimate(flops=0, bytes_accessed=4 * spread.size, transcendentals=0),
    )(spread, *waits)


def lag_body(order, *refs):
    count = len(order)
    blocks = [refs[order.index(at)] for at in range(count)]
    cosines, sines, *partial, out = refs[count:]
    stations, _, width = blocks[0].shape[-3:]
    half = width // 2
    real, imag = [], []
    for station in range(stations):
        spectra = []
        for block in blocks:
            if len(block.shape) == 4:
                spectra.append(block[0, station])
            else:
                spectra += [block[shard, 0, station] for shard in range(block.shape[0])]
        turned = jnp.concatenate(spectra, 0).T
        real.append(turned[:half])
        imag.append(turned[half:])
    lagged = jnp.dot(jnp.concatenate(real, 0), cosines[...], preferred_element_type=jnp.float32)
    lagged += jnp.dot(jnp.concatenate(imag, 0), sines[...], preferred_element_type=jnp.float32)
    if partial:
        lagged += partial[0][0, 0]
    out[0, 0] = lagged.astype(out.dtype)


def to_lags(blocks, order, cosines, sines, part, partial, kind):
    rounds, stations, freqs, width = blocks[0].shape[-4:]
    half = width // 2
    rows = sum(block.size for block in blocks) // (rounds * stations * width)
    lags = cosines.shape[1]
    step = math.gcd(stations, 8)

    def spec(block):
        if block.ndim == 4:
            return pl.BlockSpec((1, step, freqs, width), lambda turn, at: (turn, at, 0, 0))
        return pl.BlockSpec((block.shape[0], 1, step, freqs, width), lambda turn, at: (0, turn, at, 0, 0))

    table = pl.BlockSpec((rows, lags), lambda turn, at: (part, 0))
    lagged = pl.BlockSpec((1, 1, step * half, lags), lambda turn, at: (turn, 0, at, 0))
    return pl.pallas_call(
        functools.partial(lag_body, order),
        out_shape=jax.ShapeDtypeStruct((rounds, 1, stations * half, lags), kind),
        grid=(rounds, stations // step),
        in_specs=[spec(blocks[at]) for at in order] + [table] * 2 + [lagged] * len(partial),
        out_specs=lagged,
        compiler_params=pltpu.CompilerParams(vmem_limit_bytes=VMEM),
        cost_estimate=pl.CostEstimate(
            flops=2 * rounds * stations * half * 2 * rows * lags,
            bytes_accessed=2 * (rounds * stations * half * (2 * rows + lags) + 2 * rows * lags),
            transcendentals=0,
        ),
    )(*[blocks[at] for at in order], cosines, sines, *partial)


def inverse_table(band_weight, shard, odd, chunks, straight):
    bins = band_weight.shape[0]
    shards = lax.axis_size("frq")
    lags = 2 * bins
    size = bins // (shards * 2 * chunks)

    weights = band_weight.reshape(shards, 2, chunks, size)
    weights = jnp.where(odd == 0, weights[:, ::-1], weights).transpose(2, 1, 0, 3)
    backward = jnp.concatenate([weights[:, :, ::-1]] * 2, 2)
    backward = lax.dynamic_slice_in_dim(backward, shards - 1 - shard, shards, 2)
    weights = jnp.concatenate([weights[: chunks - straight], backward[chunks - straight :]], 0).reshape(bins)

    dims = (chunks, 2, shards, size)
    chunk, bundle, place, offset = (lax.broadcasted_iota(jnp.int32, dims, at) for at in range(4))
    source = jnp.where(chunk < chunks - straight, place, (shard + shards - place) % shards)
    indices = ((source * 2 + (bundle ^ 1 ^ odd)) * chunks + chunk) * size + offset
    indices = indices.reshape(bins)
    phase_index = indices[:, None] * jnp.arange(lags, dtype=jnp.int32)[None, :] % lags
    phase_angle = phase_index.astype(jnp.float32) * (2.0 * math.pi / lags)
    weighting = weights[:, None] * (1.0 / math.sqrt(bins))
    return (
        (weighting * jnp.cos(phase_angle)).astype(jnp.bfloat16),
        (-weighting * jnp.sin(phase_angle)).astype(jnp.bfloat16),
    )


def local(spectra, band_weight):
    shards = lax.axis_size("frq")
    group = lax.axis_index("grp").astype(jnp.int32)
    shard = lax.axis_index("frq").astype(jnp.int32)
    core, odd = group & 1, (group >> 1) & 1
    block = spectra[0]
    half_size = block.shape[0] // 2
    chunks = max(1, half_size // CHUNK)
    size = half_size // chunks
    straight = min(STRAIGHT, chunks)
    cosines, sines = inverse_table(band_weight, shard, odd, chunks, straight)

    def piece(source, half, chunk):
        return lax.dynamic_slice_in_dim(source, (half * chunks + chunk) * size, size, 0)

    sent, later = [], []
    source = block
    for chunk in range(chunks):
        x_piece, y_piece = piece(source, 1 - odd, chunk), piece(source, odd, chunk)
        x_piece, y_piece, source = lax.optimization_barrier((x_piece, y_piece, source))
        sent.append((y_piece, permuted(x_piece, to_x), permuted(y_piece, to_y)))
        if chunk:
            later += [x_piece, y_piece]

    spreads, blocks = [], [None] * chunks
    for chunk, (own, x_mine, y_mine) in enumerate(sent):
        scalars = jnp.stack([core, odd, odd * chunks + chunk, shard])
        x_other = permuted(x_mine, to_other_core)
        if chunk == 0:
            last = last_after(scalars, own, y_mine, later + [cosines, sines])
        else:
            last = jnp.where(odd == core, y_mine, own)
        last_other = permuted(last, to_other_core)
        is_straight = chunk >= chunks - straight
        waits = blocks[chunk - 3] if chunk >= 3 else []
        results = cross_spectra(
            scalars, block, x_mine, y_mine, x_other, last_other, waits, shards, is_straight
        )
        if is_straight:
            if spreads:
                pair = bundles_after(spreads[-1], results[:1])
                blocks[len(spreads) - 1] = [permuted(pair[0], to_x), permuted(pair[1], to_b)]
            arrived = {}
            for bundle, target in ((1, to_b), (0, to_x)):
                for distance in sorted(range(shards), key=lambda distance: -min(distance, shards - distance)):
                    at = bundle * shards + distance
                    arrived[at] = permuted_far(results[at], target, distance)
            blocks[chunk] = [arrived[at] for at in range(2 * shards)]
        else:
            spread = lax.all_to_all(results[0], "frq", split_axis=0, concat_axis=0, tiled=True)
            spreads.append(spread)
            if chunk + 1 < chunks - straight:
                blocks[chunk] = [permuted(spread[:, 0], to_x), permuted(spread[:, 1], to_b)]
    partial, part = [], 0
    if chunks == 4:
        early = blocks[0] + blocks[1]
        partial = [to_lags(early, range(len(early)), cosines, sines, 0, [], jnp.float32)]
        blocks, part = blocks[2:], 1
    beside = [at + len(sum(blocks[:-1], [])) for at in range(shards, 2 * shards)]
    over = [at - shards for at in beside]
    order = beside + list(range(over[0])) + over
    return to_lags(sum(blocks, []), order, cosines, sines, part, partial, jnp.bfloat16)


def solution(mesh):
    return jax.shard_map(
        local,
        mesh=mesh,
        in_specs=(P("grp", "frq", None, None), P()),
        out_specs=P(None, "grp", "frq", None),
        check_vma=False,
    )
```

```python
import functools
import math

import jax
import jax.numpy as jnp
from jax import lax
from jax.experimental import pallas as pl
from jax.experimental.pallas import tpu as pltpu
from jax.sharding import PartitionSpec as P

ROUNDS = 2
CHUNK = 16
STRAIGHT = 1
VMEM = 48 * 1024 * 1024
LITTLE = 8 * 1024 * 1024


def permuted(value, target):
    count = lax.axis_size("grp")
    return lax.ppermute(value, "grp", [(source, target(source) % count) for source in range(count)])


def permuted_far(value, target, distance):
    groups, shards = lax.axis_size("grp"), lax.axis_size("frq")
    return lax.ppermute(
        value,
        ("grp", "frq"),
        [
            (group * shards + shard, (target(group) % groups) * shards + (shard + distance) % shards)
            for group in range(groups)
            for shard in range(shards)
        ],
    )


def is_odd(group):
    return (group // 2) % 2


def to_x(group):
    return group ^ 2


def to_y(group):
    return group + 4 if is_odd(group) else group - 4


def to_b(group):
    return group if is_odd(group) else group + 4


def to_other_core(group):
    return group ^ 1


def cross_body(shards, step_freqs, early, straight, scalars, own, x_mine, y_mine, x_other, last_other, *refs):
    outs, stage = refs[early:-1], refs[-1]
    windows, width = own.shape[1:]
    half = width // 2
    per_shard, freqs = outs[0].shape[-3:-1]
    step = pl.program_id(0)
    first_core = scalars[0] == 0
    odd = scalars[1] == 1
    scale = 1.0 / math.sqrt(windows)
    lanes = lax.broadcasted_iota(jnp.int32, (half, width), 1)
    sign = jnp.where(lanes < half, 1.0, -1.0).astype(jnp.float32)

    def products(left, rights):
        return lax.dot_general(
            left,
            jnp.concatenate(rights, 1),
            (((0,), (0,)), ((), ())),
            preferred_element_type=jnp.float32,
        )

    for at in range(step_freqs):
        center, center_other, other = x_mine[at], x_other[at], last_other[at]
        before = jnp.where(odd, y_mine[at], own[at])
        after = jnp.where(odd, own[at], y_mine[at])
        pair = [
            products(center, [jnp.where(first_core, other, center_other), before]),
            products(after, [jnp.where(first_core, center_other, other), center]),
        ]
        for bundle, product in enumerate(pair):
            for turn in range(ROUNDS):
                part = product[:, turn * width : (turn + 1) * width]
                top, bottom = part[:half], part[half:]
                value = (top * sign + pltpu.roll(bottom, half, 1)) * scale
                base = (bundle * ROUNDS + turn) * half * freqs
                stage[pl.ds(base + step * step_freqs + at, half, stride=freqs), :] = value

    @pl.when(step == pl.num_programs(0) - 1)
    def _():
        for index in range(shards):
            shard = lax.rem(scalars[3] + index, shards) if straight else index
            for bundle in range(2):
                for turn in range(ROUNDS):
                    base = ((bundle * ROUNDS + turn) * half + shard * per_shard) * freqs
                    if straight:
                        base = pl.multiple_of(base, 8)
                    rows = stage[pl.ds(base, per_shard * freqs), :]
                    rows = rows.reshape(per_shard, freqs, width).astype(jnp.bfloat16)
                    if straight:
                        outs[bundle * shards + index][turn] = rows
                    else:
                        outs[0][index, bundle, turn] = rows


def cross_spectra(scalars, spectra, x_mine, y_mine, x_other, last_other, earlier, shards, straight):
    freqs, windows, width = x_mine.shape
    step_freqs = math.gcd(freqs, 4)
    half = width // 2
    block = (step_freqs, windows, width)
    plain = pl.BlockSpec(block, lambda step, scalars: (step, 0, 0))
    out_shape = (ROUNDS, half // shards, freqs, width)
    if not straight:
        out_shape = (shards, 2) + out_shape
    count = 2 * shards if straight else 1
    return pl.pallas_call(
        functools.partial(cross_body, shards, step_freqs, len(earlier), straight),
        out_shape=[jax.ShapeDtypeStruct(out_shape, jnp.bfloat16)] * count,
        grid_spec=pltpu.PrefetchScalarGridSpec(
            num_scalar_prefetch=1,
            grid=(freqs // step_freqs,),
            in_specs=[
                pl.BlockSpec(block, lambda step, scalars: (scalars[2] * (freqs // step_freqs) + step, 0, 0))
            ]
            + [plain] * 4
            + anywhere(len(earlier)),
            out_specs=[pl.BlockSpec(out_shape, lambda step, scalars: (0,) * len(out_shape))] * count,
            scratch_shapes=[pltpu.VMEM((2 * ROUNDS * half * freqs, width), jnp.float32)],
        ),
        compiler_params=pltpu.CompilerParams(vmem_limit_bytes=VMEM),
        cost_estimate=pl.CostEstimate(
            flops=2 * freqs * 2 * windows * width * 2 * width,
            bytes_accessed=5 * freqs * windows * width * 2 + 4 * freqs * half * width * 2,
            transcendentals=0,
        ),
    )(scalars, spectra, x_mine, y_mine, x_other, last_other, *earlier)


def anywhere(count):
    return [pl.BlockSpec(memory_space=pl.ANY)] * count


def last_body(scalars, own, y_mine, *refs):
    refs[-1][...] = jnp.where(scalars[0] == scalars[1], y_mine[...], own[...])


def last_after(scalars, own, y_mine, waits):
    return pl.pallas_call(
        last_body,
        out_shape=jax.ShapeDtypeStruct(y_mine.shape, jnp.bfloat16),
        in_specs=[pl.BlockSpec(memory_space=pltpu.SMEM)]
        + [pl.BlockSpec(memory_space=pltpu.VMEM)] * 2
        + anywhere(len(waits)),
        out_specs=pl.BlockSpec(memory_space=pltpu.VMEM),
        compiler_params=pltpu.CompilerParams(vmem_limit_bytes=LITTLE),
        cost_estimate=pl.CostEstimate(flops=0, bytes_accessed=6 * y_mine.size, transcendentals=0),
    )(scalars, own, y_mine, *waits)


def bundles_body(spread, *refs):
    for bundle in range(2):
        refs[-2 + bundle][...] = spread[:, bundle]


def bundles_after(spread, waits):
    shape = jax.ShapeDtypeStruct(spread.shape[:1] + spread.shape[2:], spread.dtype)
    return pl.pallas_call(
        bundles_body,
        out_shape=[shape] * 2,
        in_specs=[pl.BlockSpec(memory_space=pltpu.VMEM)] + anywhere(len(waits)),
        out_specs=[pl.BlockSpec(memory_space=pltpu.VMEM)] * 2,
        compiler_params=pltpu.CompilerParams(vmem_limit_bytes=LITTLE),
        cost_estimate=pl.CostEstimate(flops=0, bytes_accessed=4 * spread.size, transcendentals=0),
    )(spread, *waits)


def lag_body(order, *refs):
    count = len(order)
    blocks = [refs[order.index(at)] for at in range(count)]
    cosines, sines, out = refs[count:]
    stations, _, width = blocks[0].shape[-3:]
    half = width // 2
    real, imag = [], []
    for station in range(stations):
        spectra = []
        for block in blocks:
            if len(block.shape) == 4:
                spectra.append(block[0, station])
            else:
                spectra += [block[shard, 0, station] for shard in range(block.shape[0])]
        turned = jnp.concatenate(spectra, 0).T
        real.append(turned[:half])
        imag.append(turned[half:])
    lagged = jnp.dot(jnp.concatenate(real, 0), cosines[...], preferred_element_type=jnp.float32)
    lagged += jnp.dot(jnp.concatenate(imag, 0), sines[...], preferred_element_type=jnp.float32)
    out[0, 0] = lagged.astype(out.dtype)


def to_lags(blocks, order, cosines, sines):
    rounds, stations, freqs, width = blocks[0].shape[-4:]
    half = width // 2
    bins, lags = cosines.shape
    step = math.gcd(stations, 8)

    def spec(block):
        if block.ndim == 4:
            return pl.BlockSpec((1, step, freqs, width), lambda turn, at: (turn, at, 0, 0))
        return pl.BlockSpec((block.shape[0], 1, step, freqs, width), lambda turn, at: (0, turn, at, 0, 0))

    table = pl.BlockSpec((bins, lags), lambda turn, at: (0, 0))
    return pl.pallas_call(
        functools.partial(lag_body, order),
        out_shape=jax.ShapeDtypeStruct((rounds, 1, stations * half, lags), jnp.bfloat16),
        grid=(rounds, stations // step),
        in_specs=[spec(blocks[at]) for at in order] + [table] * 2,
        out_specs=pl.BlockSpec((1, 1, step * half, lags), lambda turn, at: (turn, 0, at, 0)),
        compiler_params=pltpu.CompilerParams(vmem_limit_bytes=VMEM),
        cost_estimate=pl.CostEstimate(
            flops=2 * rounds * stations * half * 2 * bins * lags,
            bytes_accessed=2 * (rounds * stations * half * (2 * bins + lags) + 2 * bins * lags),
            transcendentals=0,
        ),
    )(*[blocks[at] for at in order], cosines, sines)


def inverse_table(band_weight, shard, odd, chunks, straight):
    bins = band_weight.shape[0]
    shards = lax.axis_size("frq")
    lags = 2 * bins
    size = bins // (shards * 2 * chunks)

    weights = band_weight.reshape(shards, 2, chunks, size)
    weights = jnp.where(odd == 0, weights[:, ::-1], weights).transpose(2, 1, 0, 3)
    backward = jnp.concatenate([weights[:, :, ::-1]] * 2, 2)
    backward = lax.dynamic_slice_in_dim(backward, shards - 1 - shard, shards, 2)
    weights = jnp.concatenate([weights[: chunks - straight], backward[chunks - straight :]], 0).reshape(bins)

    dims = (chunks, 2, shards, size)
    chunk, bundle, place, offset = (lax.broadcasted_iota(jnp.int32, dims, at) for at in range(4))
    source = jnp.where(chunk < chunks - straight, place, (shard + shards - place) % shards)
    indices = ((source * 2 + (bundle ^ 1 ^ odd)) * chunks + chunk) * size + offset
    indices = indices.reshape(bins)
    phase_index = indices[:, None] * jnp.arange(lags, dtype=jnp.int32)[None, :] % lags
    phase_angle = phase_index.astype(jnp.float32) * (2.0 * math.pi / lags)
    weighting = weights[:, None] * (1.0 / math.sqrt(bins))
    return (
        (weighting * jnp.cos(phase_angle)).astype(jnp.bfloat16),
        (-weighting * jnp.sin(phase_angle)).astype(jnp.bfloat16),
    )


def local(spectra, band_weight):
    shards = lax.axis_size("frq")
    group = lax.axis_index("grp").astype(jnp.int32)
    shard = lax.axis_index("frq").astype(jnp.int32)
    core, odd = group & 1, (group >> 1) & 1
    block = spectra[0]
    half_size = block.shape[0] // 2
    chunks = max(1, half_size // CHUNK)
    size = half_size // chunks
    straight = min(STRAIGHT, chunks)
    cosines, sines = inverse_table(band_weight, shard, odd, chunks, straight)

    def piece(source, half, chunk):
        return lax.dynamic_slice_in_dim(source, (half * chunks + chunk) * size, size, 0)

    sent, later = [], []
    source = block
    for chunk in range(chunks):
        x_piece, y_piece = piece(source, 1 - odd, chunk), piece(source, odd, chunk)
        x_piece, y_piece, source = lax.optimization_barrier((x_piece, y_piece, source))
        sent.append((y_piece, permuted(x_piece, to_x), permuted(y_piece, to_y)))
        if chunk:
            later += [x_piece, y_piece]

    spreads, blocks = [], [None] * chunks
    for chunk, (own, x_mine, y_mine) in enumerate(sent):
        scalars = jnp.stack([core, odd, odd * chunks + chunk, shard])
        x_other = permuted(x_mine, to_other_core)
        if chunk == 0:
            last = last_after(scalars, own, y_mine, later + [cosines, sines])
        else:
            last = jnp.where(odd == core, y_mine, own)
        last_other = permuted(last, to_other_core)
        is_straight = chunk >= chunks - straight
        waits = blocks[chunk - 3] if chunk >= 3 else []
        results = cross_spectra(
            scalars, block, x_mine, y_mine, x_other, last_other, waits, shards, is_straight
        )
        if is_straight:
            if spreads:
                pair = bundles_after(spreads[-1], results[:1])
                blocks[len(spreads) - 1] = [permuted(pair[0], to_x), permuted(pair[1], to_b)]
            arrived = {}
            for bundle, target in ((1, to_b), (0, to_x)):
                for distance in sorted(range(shards), key=lambda distance: -min(distance, shards - distance)):
                    at = bundle * shards + distance
                    arrived[at] = permuted_far(results[at], target, distance)
            blocks[chunk] = [arrived[at] for at in range(2 * shards)]
        else:
            spread = lax.all_to_all(results[0], "frq", split_axis=0, concat_axis=0, tiled=True)
            spreads.append(spread)
            if chunk + 1 < chunks - straight:
                blocks[chunk] = [permuted(spread[:, 0], to_x), permuted(spread[:, 1], to_b)]
    blocks = sum(blocks, [])

    before = len(blocks) - 2 * shards * straight
    far_first = sorted(range(shards), key=lambda distance: -min(distance, shards - distance))
    order = list(range(before))
    for first in range(before, len(blocks), 2 * shards):
        order += [first + bundle * shards + distance for bundle in range(2) for distance in far_first[:-1]]
        order += [first + bundle * shards + far_first[-1] for bundle in range(2)]
    return to_lags(blocks, order, cosines, sines)


def solution(mesh):
    return jax.shard_map(
        local,
        mesh=mesh,
        in_specs=(P("grp", "frq", None, None), P()),
        out_specs=P(None, "grp", "frq", None),
        check_vma=False,
    )
```

```python
import functools
import math

import jax
import jax.numpy as jnp
from jax import lax
from jax.experimental import pallas as pl
from jax.experimental.pallas import tpu as pltpu
from jax.sharding import PartitionSpec as P

ROUNDS = 2
CHUNK = 16
STRAIGHT = 1
VMEM = 48 * 1024 * 1024
LITTLE = 8 * 1024 * 1024


def permuted(value, target):
    count = lax.axis_size("grp")
    return lax.ppermute(value, "grp", [(source, target(source) % count) for source in range(count)])


def permuted_far(value, target, distance):
    groups, shards = lax.axis_size("grp"), lax.axis_size("frq")
    return lax.ppermute(
        value,
        ("grp", "frq"),
        [
            (group * shards + shard, (target(group) % groups) * shards + (shard + distance) % shards)
            for group in range(groups)
            for shard in range(shards)
        ],
    )


def is_odd(group):
    return (group // 2) % 2


def to_x(group):
    return group ^ 2


def to_y(group):
    return group + 4 if is_odd(group) else group - 4


def to_b(group):
    return group if is_odd(group) else group + 4


def to_other_core(group):
    return group ^ 1


def cross_body(shards, step_freqs, early, straight, scalars, own, x_mine, y_mine, x_other, last_other, *refs):
    outs, stage = refs[early:-1], refs[-1]
    windows, width = own.shape[1:]
    half = width // 2
    per_shard, freqs = outs[0].shape[-3:-1]
    step = pl.program_id(0)
    first_core = scalars[0] == 0
    odd = scalars[1] == 1
    scale = 1.0 / math.sqrt(windows)
    lanes = lax.broadcasted_iota(jnp.int32, (half, width), 1)
    sign = jnp.where(lanes < half, 1.0, -1.0).astype(jnp.float32)

    def products(left, rights):
        return lax.dot_general(
            left,
            jnp.concatenate(rights, 1),
            (((0,), (0,)), ((), ())),
            preferred_element_type=jnp.float32,
        )

    for at in range(step_freqs):
        center, center_other, other = x_mine[at], x_other[at], last_other[at]
        before = jnp.where(odd, y_mine[at], own[at])
        after = jnp.where(odd, own[at], y_mine[at])
        pair = [
            products(center, [jnp.where(first_core, other, center_other), before]),
            products(after, [jnp.where(first_core, center_other, other), center]),
        ]
        for bundle, product in enumerate(pair):
            for turn in range(ROUNDS):
                part = product[:, turn * width : (turn + 1) * width]
                top, bottom = part[:half], part[half:]
                value = (top * sign + pltpu.roll(bottom, half, 1)) * scale
                base = (bundle * ROUNDS + turn) * half * freqs
                stage[pl.ds(base + step * step_freqs + at, half, stride=freqs), :] = value

    @pl.when(step == pl.num_programs(0) - 1)
    def _():
        for index in range(shards):
            shard = lax.rem(scalars[3] + index, shards) if straight else index
            for bundle in range(2):
                for turn in range(ROUNDS):
                    base = ((bundle * ROUNDS + turn) * half + shard * per_shard) * freqs
                    if straight:
                        base = pl.multiple_of(base, 8)
                    rows = stage[pl.ds(base, per_shard * freqs), :]
                    rows = rows.reshape(per_shard, freqs, width).astype(jnp.bfloat16)
                    if straight:
                        outs[bundle * shards + index][turn] = rows
                    else:
                        outs[0][index, bundle, turn] = rows


def cross_spectra(scalars, spectra, x_mine, y_mine, x_other, last_other, earlier, shards, straight):
    freqs, windows, width = x_mine.shape
    step_freqs = math.gcd(freqs, 4)
    half = width // 2
    block = (step_freqs, windows, width)
    plain = pl.BlockSpec(block, lambda step, scalars: (step, 0, 0))
    out_shape = (ROUNDS, half // shards, freqs, width)
    if not straight:
        out_shape = (shards, 2) + out_shape
    count = 2 * shards if straight else 1
    return pl.pallas_call(
        functools.partial(cross_body, shards, step_freqs, len(earlier), straight),
        out_shape=[jax.ShapeDtypeStruct(out_shape, jnp.bfloat16)] * count,
        grid_spec=pltpu.PrefetchScalarGridSpec(
            num_scalar_prefetch=1,
            grid=(freqs // step_freqs,),
            in_specs=[
                pl.BlockSpec(block, lambda step, scalars: (scalars[2] * (freqs // step_freqs) + step, 0, 0))
            ]
            + [plain] * 4
            + anywhere(len(earlier)),
            out_specs=[pl.BlockSpec(out_shape, lambda step, scalars: (0,) * len(out_shape))] * count,
            scratch_shapes=[pltpu.VMEM((2 * ROUNDS * half * freqs, width), jnp.float32)],
        ),
        compiler_params=pltpu.CompilerParams(vmem_limit_bytes=VMEM),
        cost_estimate=pl.CostEstimate(
            flops=2 * freqs * 2 * windows * width * 2 * width,
            bytes_accessed=5 * freqs * windows * width * 2 + 4 * freqs * half * width * 2,
            transcendentals=0,
        ),
    )(scalars, spectra, x_mine, y_mine, x_other, last_other, *earlier)


def anywhere(count):
    return [pl.BlockSpec(memory_space=pl.ANY)] * count


def last_body(scalars, own, y_mine, *refs):
    refs[-1][...] = jnp.where(scalars[0] == scalars[1], y_mine[...], own[...])


def last_after(scalars, own, y_mine, waits):
    return pl.pallas_call(
        last_body,
        out_shape=jax.ShapeDtypeStruct(y_mine.shape, jnp.bfloat16),
        in_specs=[pl.BlockSpec(memory_space=pltpu.SMEM)]
        + [pl.BlockSpec(memory_space=pltpu.VMEM)] * 2
        + anywhere(len(waits)),
        out_specs=pl.BlockSpec(memory_space=pltpu.VMEM),
        compiler_params=pltpu.CompilerParams(vmem_limit_bytes=LITTLE),
        cost_estimate=pl.CostEstimate(flops=0, bytes_accessed=6 * y_mine.size, transcendentals=0),
    )(scalars, own, y_mine, *waits)


def bundles_body(spread, *refs):
    for bundle in range(2):
        refs[-2 + bundle][...] = spread[:, bundle]


def bundles_after(spread, waits):
    shape = jax.ShapeDtypeStruct(spread.shape[:1] + spread.shape[2:], spread.dtype)
    return pl.pallas_call(
        bundles_body,
        out_shape=[shape] * 2,
        in_specs=[pl.BlockSpec(memory_space=pltpu.VMEM)] + anywhere(len(waits)),
        out_specs=[pl.BlockSpec(memory_space=pltpu.VMEM)] * 2,
        compiler_params=pltpu.CompilerParams(vmem_limit_bytes=LITTLE),
        cost_estimate=pl.CostEstimate(flops=0, bytes_accessed=4 * spread.size, transcendentals=0),
    )(spread, *waits)


def lag_body(order, *refs):
    count = len(order)
    blocks = [refs[order.index(at)] for at in range(count)]
    cosines, sines, out = refs[count:]
    stations, _, width = blocks[0].shape[-3:]
    half = width // 2
    real, imag = [], []
    for station in range(stations):
        spectra = []
        for block in blocks:
            if len(block.shape) == 4:
                spectra.append(block[0, station])
            else:
                spectra += [block[shard, 0, station] for shard in range(block.shape[0])]
        turned = jnp.concatenate(spectra, 0).T
        real.append(turned[:half])
        imag.append(turned[half:])
    lagged = jnp.dot(jnp.concatenate(real, 0), cosines[...], preferred_element_type=jnp.float32)
    lagged += jnp.dot(jnp.concatenate(imag, 0), sines[...], preferred_element_type=jnp.float32)
    out[0, 0] = lagged.astype(out.dtype)


def to_lags(blocks, order, cosines, sines):
    rounds, stations, freqs, width = blocks[0].shape[-4:]
    half = width // 2
    bins, lags = cosines.shape
    step = math.gcd(stations, 8)

    def spec(block):
        if block.ndim == 4:
            return pl.BlockSpec((1, step, freqs, width), lambda turn, at: (turn, at, 0, 0))
        return pl.BlockSpec((block.shape[0], 1, step, freqs, width), lambda turn, at: (0, turn, at, 0, 0))

    table = pl.BlockSpec((bins, lags), lambda turn, at: (0, 0))
    return pl.pallas_call(
        functools.partial(lag_body, order),
        out_shape=jax.ShapeDtypeStruct((rounds, 1, stations * half, lags), jnp.bfloat16),
        grid=(rounds, stations // step),
        in_specs=[spec(blocks[at]) for at in order] + [table] * 2,
        out_specs=pl.BlockSpec((1, 1, step * half, lags), lambda turn, at: (turn, 0, at, 0)),
        compiler_params=pltpu.CompilerParams(vmem_limit_bytes=VMEM),
        cost_estimate=pl.CostEstimate(
            flops=2 * rounds * stations * half * 2 * bins * lags,
            bytes_accessed=2 * (rounds * stations * half * (2 * bins + lags) + 2 * bins * lags),
            transcendentals=0,
        ),
    )(*[blocks[at] for at in order], cosines, sines)


def inverse_table(band_weight, shard, odd, chunks, straight):
    bins = band_weight.shape[0]
    shards = lax.axis_size("frq")
    lags = 2 * bins
    size = bins // (shards * 2 * chunks)

    weights = band_weight.reshape(shards, 2, chunks, size)
    weights = jnp.where(odd == 0, weights[:, ::-1], weights).transpose(2, 1, 0, 3)
    backward = jnp.concatenate([weights[:, :, ::-1]] * 2, 2)
    backward = lax.dynamic_slice_in_dim(backward, shards - 1 - shard, shards, 2)
    weights = jnp.concatenate([weights[: chunks - straight], backward[chunks - straight :]], 0).reshape(bins)

    dims = (chunks, 2, shards, size)
    chunk, bundle, place, offset = (lax.broadcasted_iota(jnp.int32, dims, at) for at in range(4))
    source = jnp.where(chunk < chunks - straight, place, (shard + shards - place) % shards)
    indices = ((source * 2 + (bundle ^ 1 ^ odd)) * chunks + chunk) * size + offset
    indices = indices.reshape(bins)
    phase_index = indices[:, None] * jnp.arange(lags, dtype=jnp.int32)[None, :] % lags
    phase_angle = phase_index.astype(jnp.float32) * (2.0 * math.pi / lags)
    weighting = weights[:, None] * (1.0 / math.sqrt(bins))
    return (
        (weighting * jnp.cos(phase_angle)).astype(jnp.bfloat16),
        (-weighting * jnp.sin(phase_angle)).astype(jnp.bfloat16),
    )


def local(spectra, band_weight):
    shards = lax.axis_size("frq")
    group = lax.axis_index("grp").astype(jnp.int32)
    shard = lax.axis_index("frq").astype(jnp.int32)
    core, odd = group & 1, (group >> 1) & 1
    block = spectra[0]
    half_size = block.shape[0] // 2
    chunks = max(1, half_size // CHUNK)
    size = half_size // chunks
    straight = min(STRAIGHT, chunks)
    cosines, sines = inverse_table(band_weight, shard, odd, chunks, straight)

    def piece(source, half, chunk):
        return lax.dynamic_slice_in_dim(source, (half * chunks + chunk) * size, size, 0)

    sent, later = [], []
    source = block
    for chunk in range(chunks):
        x_piece, y_piece = piece(source, 1 - odd, chunk), piece(source, odd, chunk)
        x_piece, y_piece, source = lax.optimization_barrier((x_piece, y_piece, source))
        sent.append((y_piece, permuted(x_piece, to_x), permuted(y_piece, to_y)))
        if chunk:
            later += [x_piece, y_piece]

    spreads, blocks = [], [None] * chunks
    for chunk, (own, x_mine, y_mine) in enumerate(sent):
        scalars = jnp.stack([core, odd, odd * chunks + chunk, shard])
        x_other = permuted(x_mine, to_other_core)
        if chunk == 0:
            last = last_after(scalars, own, y_mine, later + [cosines, sines])
        else:
            last = jnp.where(odd == core, y_mine, own)
        last_other = permuted(last, to_other_core)
        is_straight = chunk >= chunks - straight
        waits = blocks[chunk - 3] if chunk >= 3 else []
        results = cross_spectra(
            scalars, block, x_mine, y_mine, x_other, last_other, waits, shards, is_straight
        )
        if is_straight:
            if spreads:
                pair = bundles_after(spreads[-1], results[:1])
                blocks[len(spreads) - 1] = [permuted(pair[0], to_x), permuted(pair[1], to_b)]
            arrived = {}
            for bundle, target in ((1, to_b), (0, to_x)):
                for distance in sorted(range(shards), key=lambda distance: -min(distance, shards - distance)):
                    at = bundle * shards + distance
                    arrived[at] = permuted_far(results[at], target, distance)
            blocks[chunk] = [arrived[at] for at in range(2 * shards)]
        else:
            spread = lax.all_to_all(results[0], "frq", split_axis=0, concat_axis=0, tiled=True)
            spreads.append(spread)
            if chunk + 1 < chunks - straight:
                blocks[chunk] = [permuted(spread[:, 0], to_x), permuted(spread[:, 1], to_b)]
    blocks = sum(blocks, [])

    before = len(blocks) - 2 * shards * straight
    far_first = sorted(range(shards), key=lambda distance: -min(distance, shards - distance))
    order = list(range(before))
    for first in range(before, len(blocks), 2 * shards):
        order += [first + bundle * shards + distance for distance in far_first for bundle in range(2)]
    return to_lags(blocks, order, cosines, sines)


def solution(mesh):
    return jax.shard_map(
        local,
        mesh=mesh,
        in_specs=(P("grp", "frq", None, None), P()),
        out_specs=P(None, "grp", "frq", None),
        check_vma=False,
    )
```
